1024 devices in a mesh: bal: 4 (over y_hi), fsdp: 256 (over z, x, y_lo, core).
Axes of the slice: x: 4, y: 8 (y_hi: 4, y_lo: 2; y = y_hi * 2 + y_lo), z: 16, core: 2. Of those that a mesh axis runs over, the one named last changes fastest.
Arguments:
- patches: bfloat16 [256, 512, 6144], P('fsdp', 'bal'), may hold values from -6 to 6
- projection: bfloat16 [6144, 192], P('fsdp'), may hold values from -0.078125 to 0.078125
- image_ids: int32 [256, 512], P('fsdp'), may hold values from 0 to 7, never falling along the last dimension, each value on 1 to 256 neighbouring positions
- cotangent: bfloat16 [256, 512, 64], P('fsdp', 'bal'), may hold values from -6 to 6
Outputs:
- head_output: bfloat16 [256, 512, 64], P('fsdp', 'bal')
- patch_grads: bfloat16 [256, 512, 6144], P('fsdp', 'bal')
- projection_grad: float32 [6144, 192], P('fsdp')
The draws below stay inside these ranges and needn't reach their ends.
Inputs may be any that keep to these rules, and one draw needn't show every extreme that they name: `image_ids`: ids never fall along a sequence; every image of 0 to 7 is present, each with 1 to 256 patches, and one has exactly 256.
All inputs are finite; a program needn't handle non-finite values.
Results may differ from the reference program's by a relative error of at most 0.014.
Values may be sent and summed in bfloat16 or wider, within the bound.
A program may use at most 64 MiB of HBM per device.

```python
import math
import jax
import jax.numpy as jnp
import numpy as np
from jax import lax

D = 6144
HD = 64
SEQ = 512
IMAGES = 8
SEQS = 256


def shard_levels(stream_key, shape, shards, smallest, high):
    def one(dim, blocks):
        draws = jax.random.uniform(jax.random.fold_in(jax.random.fold_in(stream_key, 6), dim), (blocks,), jnp.float32, smallest / len(shards), high / len(shards))
        return jnp.repeat(jnp.exp(draws), shape[dim] // blocks).reshape((-1,) + (1,) * (len(shape) - dim - 1))

    gain = one(*shards[0])
    for cut in shards[1:]:
        gain = gain * one(*cut)
    return gain


def split_up(amount, total, bound, slope):
    portions = [(1 << 20) // math.isqrt(rank ** slope) + 1 for rank in range(2, amount + 1)]
    spare, holding = total - bound - (amount - 1), [1] * (amount - 1)
    while spare > 0:
        movable = [i for i in range(amount - 1) if holding[i] < bound]
        mass, remaining = sum([portions[i] for i in movable]), spare
        for i in movable:
            addition = min(bound - holding[i], max(1, remaining * portions[i] // mass), spare)
            holding[i] = holding[i] + addition
            spare = spare - addition
    return np.array([bound] + holding)


def ragged_sizes(rng, number_of, total, limit, skew):
    if number_of == 2:
        one = jax.random.randint(rng, (), max(1, total - limit), min(limit, total - 1) + 1)
        return jnp.stack([one, total - one])
    sizes = jnp.asarray(split_up(number_of, total, limit, skew), jnp.int32)
    pairs = (number_of - 1) // 2
    donor, taker = sizes[1:1 + 2 * pairs:2], sizes[2:2 + 2 * pairs:2]
    slack = jnp.minimum(donor - 1, limit - taker)
    moved = jax.random.randint(jax.random.fold_in(rng, 1), (pairs,), 0, 1 << 20) % (slack + 1)
    sizes = sizes.at[1:1 + 2 * pairs:2].set(donor - moved).at[2:2 + 2 * pairs:2].set(taker + moved)
    return sizes[jax.random.permutation(jax.random.fold_in(rng, 2), number_of)]


def noise(stream_key, extent, deviation, bound, cuts=(), kind=jnp.bfloat16):
    result = jax.random.normal(stream_key, extent, jnp.float32) * deviation
    if len(cuts) > 0:
        result = shard_levels(stream_key, extent, cuts, -0.22, 0.18) * result
    return jnp.clip(result, min=-bound, max=bound).astype(kind)


def setup_inputs(seed: int = 0) -> dict:
    keys = jax.random.split(jax.random.key(seed), 5)
    return {
        "patches": noise(keys[0], (SEQS, SEQ, D), 1.0, 6.0, ((0, 256), (1, 4))),
        "projection": noise(keys[1], (D, 3 * HD), D ** -0.5, 0.078125, ((0, 256),)),
        "image_ids": jax.vmap(lambda own: jnp.searchsorted(jnp.cumsum(ragged_sizes(own, IMAGES, SEQ, SEQ // 2, 2)), jnp.arange(SEQ), side="right"))(jax.random.split(keys[2], SEQS)).reshape((SEQS, SEQ)).astype(jnp.int32),
        "cotangent": noise(keys[3], (SEQS, SEQ, HD), 1.0, 6.0, ((0, 256), (1, 4))),
    }


EPSILON = 1e-06
CONTRACT_LAST = (((1,), (1,)), ((), ()))
CONTRACT_FIRST = (((0,), (0,)), ((), ()))

def norm_rows(values):
    centred = values - lax.optimization_barrier(jnp.mean(values, axis=-1, keepdims=True))
    inverse = lax.rsqrt(lax.optimization_barrier(jnp.mean(centred * centred, axis=-1, keepdims=True)) + EPSILON)
    return (centred * inverse, inverse)

def norm_backward(upstream, normal, inverse):
    shifted = upstream - lax.optimization_barrier(jnp.mean(upstream, axis=-1, keepdims=True))
    return inverse * (shifted - normal * lax.optimization_barrier(jnp.mean(upstream * normal, axis=-1, keepdims=True)))

def one_sequence(patch_rows, image_row, upstream, projection):
    head_width = projection.shape[1] // 3
    factor = 1.0 / math.sqrt(head_width)
    normal_x, inverse_x = norm_rows(patch_rows.astype(jnp.float32))
    normed = normal_x.astype(jnp.bfloat16)
    joined_rows = jnp.dot(normed, projection, preferred_element_type=jnp.float32)
    normal_q, inverse_q = norm_rows(joined_rows[:, :head_width])
    normal_k, inverse_k = norm_rows(joined_rows[:, head_width:2 * head_width])
    query_rows = normal_q.astype(jnp.bfloat16)
    key_rows = normal_k.astype(jnp.bfloat16)
    value_rows = joined_rows[:, 2 * head_width:].astype(jnp.bfloat16)
    same_image = image_row[:, None] == image_row[None, :]
    scores = lax.dot_general(query_rows, key_rows, CONTRACT_LAST, preferred_element_type=jnp.float32) * factor
    exponent = jnp.where(same_image, jnp.exp(scores), 0.0)
    denominator = lax.optimization_barrier(jnp.sum(exponent, axis=-1))
    probs = exponent.astype(jnp.bfloat16)
    attended = jnp.dot(probs, value_rows, preferred_element_type=jnp.float32) / denominator[:, None]
    upstream_f = upstream.astype(jnp.float32)
    scaled_grad = (upstream_f / denominator[:, None]).astype(jnp.bfloat16)
    correction = lax.optimization_barrier(jnp.sum(upstream_f * attended, axis=-1)) / denominator
    prob_grad = lax.dot_general(scaled_grad, value_rows, CONTRACT_LAST, preferred_element_type=jnp.float32)
    score_grad = (probs.astype(jnp.float32) * (prob_grad - correction[:, None])).astype(jnp.bfloat16)
    query_grad = jnp.dot(score_grad, key_rows, preferred_element_type=jnp.float32) * factor
    key_grad = lax.dot_general(score_grad, query_rows, CONTRACT_FIRST, preferred_element_type=jnp.float32) * factor
    value_grad = lax.dot_general(probs, scaled_grad, CONTRACT_FIRST, preferred_element_type=jnp.float32)
    joined_grad = jnp.concatenate([norm_backward(query_grad, normal_q, inverse_q), norm_backward(key_grad, normal_k, inverse_k), value_grad], axis=-1).astype(jnp.bfloat16)
    normed_grad = lax.dot_general(joined_grad, projection, CONTRACT_LAST, preferred_element_type=jnp.float32)
    patch_grad = norm_backward(normed_grad, normal_x, inverse_x).astype(jnp.bfloat16)
    term = lax.dot_general(normed, joined_grad, CONTRACT_FIRST, preferred_element_type=jnp.float32)
    return (attended.astype(jnp.bfloat16), patch_grad, term)

def reference(patches, projection, image_ids, cotangent):

    def advance(carry, item):
        rows_in, ids_in, grad_in = item
        output_rows, patch_grad, term = one_sequence(rows_in, ids_in, grad_in, projection)
        return (carry + term, (output_rows, patch_grad))
    initial = jnp.zeros((projection.shape[0], projection.shape[1]), jnp.float32)
    total_grad, (outputs, grads) = lax.scan(advance, initial, (patches, image_ids, cotangent))
    return (outputs, grads, total_grad)
```

```python
import functools
import math

import jax
import jax.numpy as jnp
from jax import lax
from jax.experimental import pallas as pl
from jax.experimental.pallas import tpu as pltpu
from jax.sharding import PartitionSpec as P

EPSILON = 1e-06
MESH = pl.DeviceIdType.MESH
F32 = jnp.float32
BF16 = jnp.bfloat16
NT = (((1,), (1,)), ((), ()))
TN = (((0,), (0,)), ((), ()))

D = 6144
HALF = D // 2
ROWS = 128
HD = 64
BLK = 384


def device(z, x, y, c):
    return (y // 2, ((z * 4 + x) * 2 + y % 2) * 2 + c)


def dot(a, b):
    return jnp.dot(a, b, preferred_element_type=F32)


def dot_nt(a, b):
    return lax.dot_general(a, b, NT, preferred_element_type=F32)


def dot_tn(a, b):
    return lax.dot_general(a, b, TN, preferred_element_type=F32)


def kernel(
    x_ref, w_ref, ids_ref, cot_ref,
    out_ref, pg_ref, gw_ref,
    nfull, nall, ntr, stats, zland, wbuf, jpart, jrecv,
    qk_all, v_all, cot_all, jbuf, gbuf, xland, ysend, yland, zsend, zland2, fsend, fland, ngs,
    local_sem, nsem, zs_sem, zr_sem, xs_sem, xr_sem, ys_sem, yr_sem, ws_sem, wr_sem,
    jsem, qs_sem, qr_sem, gsem, gxs_sem, gxr_sem, gys_sem, gyr_sem, gzs_sem, gzr_sem, fs_sem, fr_sem,
):
    h = lax.axis_index("bal")
    f = lax.axis_index("fsdp")
    c = f % 2
    l = (f // 2) % 2
    x = (f // 4) % 4
    z = f // 16
    y = 2 * h + l
    zhalf = z // 8
    zlow = z % 8
    other = device(z, x, y, 1 - c)
    home = zhalf == c
    own = jnp.logical_and(home, z % 4 == h)

    def remote(src, dst, ssem, rsem, dev):
        return pltpu.make_async_remote_copy(
            src_ref=src, dst_ref=dst, send_sem=ssem, recv_sem=rsem, device_id=dev, device_id_type=MESH
        )

    bar = pltpu.get_barrier_semaphore()

    def signal(dev):
        pl.semaphore_signal(bar, inc=1, device_id=dev, device_id_type=MESH)

    for zl in range(8):
        for cs in range(2):
            me = jnp.logical_and(c * 8 + zl == z, c == cs)

            @pl.when(jnp.logical_not(me))
            def _():
                signal(device(c * 8 + zl, x, y, cs))

    @pl.when(own)
    def _():
        for k in range(1, 16):
            signal(device((z + k) % 16, x, y, c))

    @pl.when(jnp.logical_not(own))
    def _():
        signal(device(z, x, 2 * (z % 4) + l, zhalf))

    signal(other)
    for k in range(1, 4):
        signal(device(z, (x + k) % 4, y, c))
    for k in range(1, 8):
        signal(device(z, x, (y + k) % 8, c))
    expected = (
        15 + jnp.where(home, 0, 1) + jnp.where(own, 8, 2) + 1 + 3 + 7
    )

    def norm_body(i, carry):
        rows = pl.ds(pl.multiple_of(i * 16, 16), 16)
        v = x_ref[rows, :].astype(F32)
        mean = jnp.mean(v, axis=-1, keepdims=True)
        cen = v - mean
        inv = lax.rsqrt(jnp.mean(cen * cen, axis=-1, keepdims=True) + EPSILON)
        nfull[rows, :] = (cen * inv).astype(BF16)
        stats[0, rows, :] = jnp.broadcast_to(mean, (16, 128))
        stats[1, rows, :] = jnp.broadcast_to(inv, (16, 128))
        return carry

    lax.fori_loop(0, ROWS // 16, norm_body, 0)
    cot_all[0] = cot_ref[...]

    pl.semaphore_wait(bar, expected)

    zcopies = []
    for k in (8, 7, 9, 6, 10, 5, 11, 4, 12, 3, 13, 2, 14, 1, 15):
        cp = remote(w_ref, zland.at[zlow, c], zs_sem.at[k], zr_sem.at[zlow, c], device((z + k) % 16, x, y, zhalf))
        cp.start()
        zcopies.append(cp)
    zcross = remote(w_ref, zland.at[zlow, c], zs_sem.at[0], zr_sem.at[zlow, c], other)

    @pl.when(jnp.logical_not(home))
    def _():
        zcross.start()

    @pl.when(home)
    def _():
        zland[zlow, c] = w_ref[...]

    mine = pl.ds(pl.multiple_of(c * ROWS, ROWS), ROWS)
    ncopy = remote(
        nfull.at[:, pl.ds(pl.multiple_of((1 - c) * HALF, HALF), HALF)], nall.at[mine], nsem.at[0], nsem.at[1], other
    )
    ncopy.start()
    nlocal = pltpu.make_async_copy(
        nfull.at[:, pl.ds(pl.multiple_of(c * HALF, HALF), HALF)], nall.at[mine], local_sem
    )
    nlocal.start()
    ccopies = []
    for k in range(1, 4):
        cp = remote(cot_all.at[0], cot_all.at[4 - k], qs_sem.at[2, k], qr_sem.at[2, k], device(z, x, (y + 2 * k) % 8, c))
        cp.start()
        ccopies.append(cp)
    nlocal.wait()
    ncopy.wait()

    def tr_body(i, carry):
        col = pl.ds(pl.multiple_of(i * BLK, BLK), BLK)
        ntr[col, :] = nall[:, col].T
        return carry

    lax.fori_loop(0, 8, tr_body, 0)

    xcopies = []
    for zz in range(4):
        halves = []
        for zl in (zz, zz + 4):
            for cs in range(2):
                me = jnp.logical_and(c * 8 + zl == z, c == cs)

                @pl.when(jnp.logical_not(me))
                def _():
                    remote(w_ref, zland.at[zl, cs], zs_sem.at[0], zr_sem.at[zl, cs], other).wait_recv()

            halves.append(
                jnp.concatenate([zland[zl, 0].astype(F32), zland[zl, 1].astype(F32)], axis=0)
            )
        a, b = halves
        wbuf[c, zz, 0, x, l] = a[:, :128].astype(BF16)
        wbuf[c, zz, 1, x, l] = b[:, :128].astype(BF16)
        wbuf[c, zz, 2, x, l] = jnp.concatenate([a[:, 128:], b[:, 128:]], axis=1).astype(BF16)
        piece = wbuf.at[c, zz, :, x, l]
        for k in (2, 1, 3):
            cp = remote(piece, piece, xs_sem.at[zz, k], xr_sem.at[zz, k], device(z, (x + k) % 4, y, c))
            cp.start()
            xcopies.append(cp)

    order = (0, 2, 1, 3)
    ycopies = {}
    for zz in order:
        for k in range(1, 4):
            src = wbuf.at[c, zz, :, (x + 4 - k) % 4, l]
            remote(src, src, xs_sem.at[zz, k], xr_sem.at[zz, k], other).wait_recv()
        piece = wbuf.at[c, zz, :, :, l]
        step = 1 if zz < 2 else 7
        cp = remote(piece, piece, ys_sem.at[zz], yr_sem.at[zz], device(z, x, (y + step) % 8, c))
        cp.start()
        ycopies[zz] = cp

    wcopies = []
    acc_a = jnp.zeros((2 * ROWS, 256), F32)
    acc_b = jnp.zeros((2 * ROWS, 256), F32)
    for zz in order:
        dst = wbuf.at[c, zz, :, :, 1 - l]
        remote(dst, dst, ys_sem.at[zz], yr_sem.at[zz], other).wait_recv()
        cp = remote(wbuf.at[c, zz], wbuf.at[c, zz], ws_sem.at[zz], wr_sem.at[zz], other)
        cp.start()
        wcopies.append(cp)
        w0 = wbuf[c, zz, 0].reshape(BLK, 128)
        w1 = wbuf[c, zz, 1].reshape(BLK, 128)
        w2 = wbuf[c, zz, 2].reshape(BLK, 128)
        na = nall[:, zz * BLK : (zz + 1) * BLK]
        nb = nall[:, (zz + 4) * BLK : (zz + 5) * BLK]
        acc_a += dot(na, jnp.concatenate([w0, w2], axis=1))
        acc_b += dot(nb, jnp.concatenate([w1, w2], axis=1))
    jq = acc_a[:, :128] + acc_b[:, :128]
    jv = acc_a[:, 128:192] + acc_b[:, 192:]
    for i in range(2):
        jpart[i, :, :128] = jq[i * ROWS : (i + 1) * ROWS]
        jpart[i, :, 128:] = jv[i * ROWS : (i + 1) * ROWS]
    jcopy = remote(jpart.at[1 - c], jrecv, jsem.at[0], jsem.at[1], other)
    jcopy.start()
    jcopy.wait_recv()
    joined = jpart[c] + jrecv[...]

    def norm_rows(values):
        centred = values - jnp.mean(values, axis=-1, keepdims=True)
        inverse = lax.rsqrt(jnp.mean(centred * centred, axis=-1, keepdims=True) + EPSILON)
        return centred * inverse, inverse

    normal_q, inverse_q = norm_rows(joined[:, :HD])
    normal_k, inverse_k = norm_rows(joined[:, HD : 2 * HD])
    value = joined[:, 2 * HD :]
    qk_all[0] = jnp.concatenate([normal_q, normal_k], axis=1).astype(BF16)
    v_all[0] = jnp.concatenate([value[:64], value[64:]], axis=1).astype(BF16)
    qcopies = []
    for k in (2, 1, 3):
        for i, buf in enumerate((qk_all, v_all)):
            cp = remote(
                buf.at[0], buf.at[4 - k], qs_sem.at[i, k], qr_sem.at[i, k], device(z, x, (y + 2 * k) % 8, c)
            )
            cp.start()
            qcopies.append(cp)
    id_rows = [
        ids_ref[:, pl.ds(pl.multiple_of(((h + r) % 4) * ROWS, ROWS), ROWS)].astype(F32) for r in range(4)
    ]
    id_row = jnp.concatenate(id_rows, axis=1)
    id_cols = [jnp.broadcast_to(r, (128, 128)).T[:, :1] for r in id_rows]
    for cp in ccopies + qcopies:
        cp.wait_recv()

    qs, ks, vs, cots = [], [], [], []
    for r in range(4):
        both = qk_all[r].astype(F32)
        qs.append(both[:, :HD].astype(BF16))
        ks.append(both[:, HD:].astype(BF16))
        packed = v_all[r].astype(F32)
        vs.append(jnp.concatenate([packed[:, :HD], packed[:, HD:]], axis=0).astype(BF16))
        cots.append(cot_all[r].astype(F32))
    k_whole = jnp.concatenate(ks, axis=0)
    v_whole = jnp.concatenate(vs, axis=0)
    factor = 1.0 / math.sqrt(HD)
    key_grad = jnp.zeros((ROWS, HD), F32)
    value_grad = jnp.zeros((ROWS, HD), F32)
    query_grad = None
    for r in range(4):
        scores = dot_nt(qs[r], k_whole) * factor
        expo = jnp.where(id_cols[r] == id_row, jnp.exp(scores), 0.0)
        denom = jnp.sum(expo, axis=-1, keepdims=True)
        probs = expo.astype(BF16)
        attended = dot(probs, v_whole) / denom
        scaled = (cots[r] / denom).astype(BF16)
        correction = jnp.sum(cots[r] * attended, axis=-1, keepdims=True) / denom
        if r == 0:
            out_ref[...] = attended.astype(BF16)
            pgrad = dot_nt(scaled, v_whole)
            sgrad = (probs.astype(F32) * (pgrad - correction)).astype(BF16)
            query_grad = dot(sgrad, k_whole) * factor
            sgrad = sgrad[:, :ROWS]
        else:
            pgrad = dot_nt(scaled, vs[0])
            sgrad = (probs[:, :ROWS].astype(F32) * (pgrad - correction)).astype(BF16)
        key_grad += dot_tn(sgrad, qs[r])
        value_grad += dot_tn(probs[:, :ROWS], scaled)
    key_grad = key_grad * factor

    def norm_backward(upstream, normal, inverse):
        shifted = upstream - jnp.mean(upstream, axis=-1, keepdims=True)
        return inverse * (shifted - normal * jnp.mean(upstream * normal, axis=-1, keepdims=True))

    zero = jnp.zeros((ROWS, HD), F32)
    jbuf[c, 0] = jnp.concatenate(
        [norm_backward(query_grad, normal_q, inverse_q), norm_backward(key_grad, normal_k, inverse_k)], axis=1
    ).astype(BF16)
    jbuf[c, 1] = jnp.concatenate([value_grad, zero], axis=1).astype(BF16)
    jbuf[c, 2] = jnp.concatenate([zero, value_grad], axis=1).astype(BF16)
    gcopy = remote(jbuf.at[c], jbuf.at[c], gsem.at[0], gsem.at[1], other)
    gcopy.start()
    theirs = jbuf.at[1 - c]
    remote(theirs, theirs, gsem.at[0], gsem.at[1], other).wait_recv()

    jplanes = [jnp.concatenate([jbuf[0, i], jbuf[1, i]], axis=0) for i in range(3)]
    ja = jnp.concatenate([jplanes[0], jplanes[1]], axis=1)
    jb = jnp.concatenate([jplanes[0], jplanes[2]], axis=1)
    gxcopies = []
    for t in range(4):
        zz = (h + t) % 4
        ga = dot(ntr[pl.ds(pl.multiple_of(zz * BLK, BLK), BLK), :], ja)
        gb = dot(ntr[pl.ds(pl.multiple_of((zz + 4) * BLK, BLK), BLK), :], jb)
        gbuf[zz, 0] = ga[:, :128].astype(BF16).reshape(4, 2, 48, 128)
        gbuf[zz, 1] = gb[:, :128].astype(BF16).reshape(4, 2, 48, 128)
        gbuf[zz, 2] = (ga[:, 128:] + gb[:, 128:]).astype(BF16).reshape(4, 2, 48, 128)
        for k in (2, 1, 3):
            cp = remote(
                gbuf.at[zz, :, (x + k) % 4], xland.at[t, k - 1], gxs_sem.at[t, k], gxr_sem.at[t, k],
                device(z, (x + k) % 4, y, c),
            )
            cp.start()
            gxcopies.append(cp)

    for cp in wcopies:
        cp.wait_send()
    for zz in order:
        dst = wbuf.at[1 - c, zz]
        remote(dst, dst, ws_sem.at[zz], wr_sem.at[zz], other).wait_recv()
    jown_a = jnp.concatenate([jbuf[c, 0], jbuf[c, 1]], axis=1)
    jown_b = jnp.concatenate([jbuf[c, 0], jbuf[c, 2]], axis=1)

    def pg_first(i, carry):
        s1, s2 = carry
        half = i // 4
        zz = i % 4
        w2 = wbuf[half, zz, 2].reshape(BLK, 128)
        mean = stats[0]
        inv = stats[1]
        for ab in range(2):
            wab = wbuf[half, zz, ab].reshape(BLK, 128)
            ng = dot_nt(jown_a if ab == 0 else jown_b, jnp.concatenate([wab, w2], axis=1))
            base = (half * 8 + zz + 4 * ab) * BLK
            for j in range(3):
                col = pl.ds(pl.multiple_of(base + j * 128, 128), 128)
                g = ng[:, j * 128 : (j + 1) * 128]
                hx = (x_ref[:, col].astype(F32) - mean) * inv
                ngs[:, col] = g
                s1 = s1 + g
                s2 = s2 + g * hx
        return s1, s2

    s1 = jnp.zeros((ROWS, 128), F32)
    s2 = s1
    for i in range(8):
        s1, s2 = pg_first(i, (s1, s2))
    m1 = jnp.broadcast_to(jnp.sum(s1, axis=-1, keepdims=True) * (1.0 / D), (ROWS, 128))
    m2 = jnp.broadcast_to(jnp.sum(s2, axis=-1, keepdims=True) * (1.0 / D), (ROWS, 128))
    stats[2] = m1
    stats[3] = m2

    gycopies = []
    for t in range(4):
        zz = (h + t) % 4
        total = gbuf[zz, :, x].astype(F32)
        for k in range(1, 4):
            dst = xland.at[t, k - 1]
            remote(dst, dst, gxs_sem.at[t, k], gxr_sem.at[t, k], other).wait_recv()
            total = total + xland[t, k - 1].astype(F32)
        ysend[t] = total.astype(BF16)
        for e in range(2):
            if t == 0 and e == 0:
                continue
            lt = (l + e) % 2
            yt = 2 * zz + lt
            slot = (y - yt + 8) % 8
            cp = remote(
                ysend.at[t, :, lt], yland.at[slot], gys_sem.at[t, e], gyr_sem.at[slot], device(z, x, yt, c)
            )
            cp.start()
            gycopies.append(cp)

    total = ysend[0, :, l].astype(F32)
    for k in range(1, 8):
        dst = yland.at[k]
        remote(dst, dst, gys_sem.at[0, 1], gyr_sem.at[k], other).wait_recv()
        total = total + yland[k].astype(F32)
    tb = total.astype(BF16)
    zsend[0] = tb[0]
    zsend[1] = tb[2]
    zsend[2] = tb[1]
    zsend[3] = tb[2]
    gzcopies = []
    for i in range(2):
        zt = c * 8 + h + 4 * i
        cp = remote(
            zsend.at[pl.ds(2 * i, 2)], zland2.at[z], gzs_sem.at[i], gzr_sem.at[z], device(zt, x, y, c)
        )
        gzcopies.append((zt, cp))

        @pl.when(zt != z)
        def _():
            cp.start()

    def pg_second(i, carry):
        mean = stats[0]
        inv = stats[1]
        m1 = stats[2]
        m2 = stats[3]
        for j in range(3):
            col = pl.ds(pl.multiple_of(i * BLK + j * 128, 128), 128)
            hx = (x_ref[:, col].astype(F32) - mean) * inv
            pg_ref[:, col] = (inv * (ngs[:, col] - m1 - hx * m2)).astype(BF16)
        return carry

    lax.fori_loop(0, 16, pg_second, 0)

    fcopies = []
    for dh in range(4):
        for dc in range(2):
            if dh == 0 and dc == 0:
                continue
            ct = (c + dc) % 2
            fcopies.append(
                remote(
                    fsend.at[ct], fland, fs_sem.at[2 * dh + dc], fr_sem, device(z, x, (y + 2 * dh) % 8, ct)
                )
            )

    @pl.when(own)
    def _():
        second = zlow // 4
        total = zsend[pl.ds(2 * second, 2)].astype(F32)
        for k in (1, 15, 2, 14, 3, 13, 4, 12, 5, 11, 6, 10, 7, 9, 8):
            dst = zland2.at[(z + k) % 16]
            remote(dst, dst, gzs_sem.at[0], gzr_sem.at[(z + k) % 16], other).wait_recv()
            total = total + zland2[(z + k) % 16].astype(F32)
        pair = total[1]
        mine_v = jnp.where(second == 0, pair[:, :HD], pair[:, HD:])
        whole = jnp.concatenate([total[0], mine_v], axis=1)
        fsend[0] = whole[:24]
        fsend[1] = whole[24:]
        for cp in fcopies:
            cp.start()
        gw_ref[...] = fsend[c]
        for cp in fcopies:
            cp.wait_send()

    @pl.when(jnp.logical_not(own))
    def _():
        remote(fland, fland, fs_sem.at[0], fr_sem, other).wait_recv()
        gw_ref[...] = fland[...]

    for cp in zcopies:
        cp.wait_send()

    @pl.when(jnp.logical_not(home))
    def _():
        zcross.wait_send()

    jcopy.wait_send()
    gcopy.wait_send()
    for cp in xcopies + list(ycopies.values()) + ccopies + qcopies + gxcopies + gycopies:
        cp.wait_send()
    for zt, cp in gzcopies:

        @pl.when(zt != z)
        def _():
            cp.wait_send()


def per_device(patches, projection, image_ids, cotangent):
    dma = pltpu.SemaphoreType.DMA
    vmem = pl.BlockSpec(memory_space=pltpu.VMEM)
    scratch = [
        pltpu.VMEM((ROWS, D), BF16),
        pltpu.VMEM((2 * ROWS, HALF), BF16),
        pltpu.VMEM((HALF, 2 * ROWS), BF16),
        pltpu.VMEM((4, ROWS, 128), F32),
        pltpu.VMEM((8, 2, 24, 192), BF16),
        pltpu.VMEM((2, 4, 3, 4, 2, 48, 128), BF16),
        pltpu.VMEM((2, ROWS, 192), F32),
        pltpu.VMEM((ROWS, 192), F32),
        pltpu.VMEM((4, ROWS, 128), BF16),
        pltpu.VMEM((4, 64, 128), BF16),
        pltpu.VMEM((4, ROWS, HD), BF16),
        pltpu.VMEM((2, 3, ROWS, 128), BF16),
        pltpu.VMEM((4, 3, 4, 2, 48, 128), BF16),
        pltpu.VMEM((4, 3, 3, 2, 48, 128), BF16),
        pltpu.VMEM((4, 3, 2, 48, 128), BF16),
        pltpu.VMEM((8, 3, 48, 128), BF16),
        pltpu.VMEM((4, 48, 128), BF16),
        pltpu.VMEM((16, 2, 48, 128), BF16),
        pltpu.VMEM((2, 24, 192), F32),
        pltpu.VMEM((24, 192), F32),
        pltpu.VMEM((ROWS, D), F32),
        dma,
        dma((2,)),
        dma((16,)), dma((8, 2)),
        dma((4, 4)), dma((4, 4)),
        dma((4,)), dma((4,)),
        dma((4,)), dma((4,)),
        dma((2,)),
        dma((3, 4)), dma((3, 4)),
        dma((2,)),
        dma((4, 4)), dma((4, 4)),
        dma((4, 2)), dma((8,)),
        dma((2,)), dma((16,)),
        dma((8,)), dma,
    ]
    out, pg, gw = pl.pallas_call(
        kernel,
        out_shape=(
            jax.ShapeDtypeStruct((ROWS, HD), BF16),
            jax.ShapeDtypeStruct((ROWS, D), BF16),
            jax.ShapeDtypeStruct((24, 192), F32),
        ),
        in_specs=[vmem] * 4,
        out_specs=(vmem,) * 3,
        scratch_shapes=scratch,
        compiler_params=pltpu.CompilerParams(
            collective_id=0, has_side_effects=True, vmem_limit_bytes=48 * 2**20
        ),
        name="head",
    )(patches[0], projection, image_ids, cotangent[0])
    return out[None], pg[None], gw


def solution(mesh):
    in_specs = (P("fsdp", "bal", None), P("fsdp", None), P("fsdp", None), P("fsdp", "bal", None))
    out_specs = (P("fsdp", "bal", None), P("fsdp", "bal", None), P("fsdp", None))
    return jax.shard_map(
        per_device, mesh=mesh, in_specs=in_specs, out_specs=out_specs, check_vma=False
    )
```

```python
import functools
import math

import jax
import jax.numpy as jnp
from jax import lax
from jax.experimental import pallas as pl
from jax.experimental.pallas import tpu as pltpu
from jax.sharding import PartitionSpec as P

EPSILON = 1e-06
MESH = pl.DeviceIdType.MESH
F32 = jnp.float32
BF16 = jnp.bfloat16
NT = (((1,), (1,)), ((), ()))
TN = (((0,), (0,)), ((), ()))

D = 6144
HALF = D // 2
ROWS = 128
HD = 64
BLK = 384


def device(z, x, y, c):
    return (y // 2, ((z * 4 + x) * 2 + y % 2) * 2 + c)


def dot(a, b):
    return jnp.dot(a, b, preferred_element_type=F32)


def dot_nt(a, b):
    return lax.dot_general(a, b, NT, preferred_element_type=F32)


def dot_tn(a, b):
    return lax.dot_general(a, b, TN, preferred_element_type=F32)


def kernel(
    x_hbm, w_hbm, ids_hbm, cot_hbm,
    out_ref, pg_ref, gw_ref,
    x_ref, w_ref, ids_ref, wpack, relay, msend, in_sem, nfull, nall, ntr, stats, zland, wbuf, jpart, jrecv,
    qk_all, v_all, cot_all, jbuf, gbuf, xland, ysend, yland, zsend, zland2, fsend, fland, ngs,
    local_sem, nsem, zs_sem, zr_sem, xs_sem, xr_sem, ys_sem, yr_sem, ws_sem, wr_sem,
    jsem, qs_sem, qr_sem, gsem, gxs_sem, gxr_sem, gys_sem, gyr_sem, gzs_sem, gzr_sem, fs_sem, fr_sem,
):
    h = lax.axis_index("bal")
    f = lax.axis_index("fsdp")
    c = f % 2
    l = (f // 2) % 2
    x = (f // 4) % 4
    z = f // 16
    y = 2 * h + l
    zhalf = z // 8
    zlow = z % 8
    other = device(z, x, y, 1 - c)
    home = zhalf == c
    own = jnp.logical_and(home, zlow // 2 == h)

    def remote(src, dst, ssem, rsem, dev):
        return pltpu.make_async_remote_copy(
            src_ref=src, dst_ref=dst, send_sem=ssem, recv_sem=rsem, device_id=dev, device_id_type=MESH
        )

    loads = [
        pltpu.make_async_copy(x_hbm.at[pl.ds(i * 32, 32)], x_ref.at[pl.ds(i * 32, 32)], in_sem.at[i]) for i in range(4)
    ]
    w_load = pltpu.make_async_copy(w_hbm, w_ref, in_sem.at[4])
    ids_load = pltpu.make_async_copy(ids_hbm, ids_ref, in_sem.at[5])
    cot_load = pltpu.make_async_copy(cot_hbm, cot_all.at[0], in_sem.at[6])
    for cp in [w_load, *loads, ids_load, cot_load]:
        cp.start()

    bar = pltpu.get_barrier_semaphore()

    def signal(dev):
        pl.semaphore_signal(bar, inc=1, device_id=dev, device_id_type=MESH)

    for zl in range(8):
        for cs in range(2):
            me = jnp.logical_and(c * 8 + zl == z, c == cs)

            @pl.when(jnp.logical_not(me))
            def _():
                signal(device(c * 8 + zl, x, y, cs))

    @pl.when(own)
    def _():
        for k in range(1, 16):
            signal(device((z + k) % 16, x, y, c))

    @pl.when(jnp.logical_not(own))
    def _():
        signal(device(z, x, 2 * (zlow // 2) + l, zhalf))

    signal(other)
    for k in range(1, 4):
        signal(device(z, (x + k) % 4, y, c))
    for k in range(1, 8):
        signal(device(z, x, (y + k) % 8, c))
    expected = (
        15 + jnp.where(home, 0, 1) + jnp.where(own, 8, 2) + 1 + 3 + 7
    )

    def norm_body(i, carry):
        rows = pl.ds(pl.multiple_of(i * 16, 16), 16)
        v = x_ref[rows, :].astype(F32)
        mean = jnp.mean(v, axis=-1, keepdims=True)
        cen = v - mean
        inv = lax.rsqrt(jnp.mean(cen * cen, axis=-1, keepdims=True) + EPSILON)
        nfull[rows, :] = (cen * inv).astype(BF16)
        stats[0, rows, :] = jnp.broadcast_to(mean, (16, 128))
        stats[1, rows, :] = jnp.broadcast_to(inv, (16, 128))
        return carry

    w_load.wait()
    wf = w_ref[...].astype(F32)
    wv = wf[:, 128:]
    wpack[...] = jnp.concatenate(
        [wf[:, :128], jnp.concatenate([wv[:16], jnp.concatenate([wv[16:], jnp.zeros((8, HD), F32)], axis=0)], axis=1)],
        axis=0,
    ).astype(BF16)
    for i in range(4):
        loads[i].wait()
        lax.fori_loop(2 * i, 2 * i + 2, norm_body, 0)
    ids_load.wait()
    cot_load.wait()

    pl.semaphore_wait(bar, expected)

    zcopies = []
    for k in (1, 15, 2, 14, 3, 13, 4, 12, 5, 11, 6, 10, 7, 9, 8):
        cp = remote(wpack, zland.at[zlow, c], zs_sem.at[k], zr_sem.at[zlow, c], device((z + k) % 16, x, y, zhalf))
        cp.start()
        zcopies.append(cp)
    zcross = remote(wpack, zland.at[zlow, c], zs_sem.at[0], zr_sem.at[zlow, c], other)

    @pl.when(jnp.logical_not(home))
    def _():
        zcross.start()

    @pl.when(home)
    def _():
        zland[zlow, c] = wpack[...]

    mine = pl.ds(pl.multiple_of(c * ROWS, ROWS), ROWS)
    ncopy = remote(
        nfull.at[:, pl.ds(pl.multiple_of((1 - c) * HALF, HALF), HALF)], nall.at[mine], nsem.at[0], nsem.at[1], other
    )
    ncopy.start()
    nlocal = pltpu.make_async_copy(
        nfull.at[:, pl.ds(pl.multiple_of(c * HALF, HALF), HALF)], nall.at[mine], local_sem
    )
    nlocal.start()
    ccopies = []
    for k in range(1, 4):
        cp = remote(cot_all.at[0], cot_all.at[4 - k], qs_sem.at[2, k], qr_sem.at[2, k], device(z, x, (y + 2 * k) % 8, c))
        cp.start()
        ccopies.append(cp)
    nlocal.wait()
    ncopy.wait()

    def tr_body(i, carry):
        col = pl.ds(pl.multiple_of(i * BLK, BLK), BLK)
        ntr[col, :] = nall[:, col].T
        return carry

    lax.fori_loop(0, 8, tr_body, 0)

    near = []
    for zz in range(4):
        gap = (z // 2 + 8 - (4 * c + zz)) % 8
        near.append(jnp.minimum(gap, 8 - gap) * 4 + zz)
    ranks = [sum((near[j] < near[i]).astype(jnp.int32) for j in range(4) if j != i) for i in range(4)]
    order = [sum(jnp.where(ranks[i] == t, i, 0) for i in range(4)) for t in range(4)]

    def shard(zl, cs):
        me = jnp.logical_and(c * 8 + zl == z, c == cs)

        @pl.when(jnp.logical_not(me))
        def _():
            remote(wpack, zland.at[zl, cs], zs_sem.at[0], zr_sem.at[zl, cs], other).wait_recv()

        return zland[zl, cs].astype(F32)

    xcopies = []
    ycopies = []
    wcopies = []

    def along_x(t):
        zz = order[t]
        heads, values = [], []
        for zl in (2 * zz, 2 * zz + 1):
            parts = [shard(zl, 0), shard(zl, 1)]
            heads.append(jnp.concatenate([p[:24] for p in parts], axis=0))
            values.append(
                jnp.concatenate([q for p in parts for q in (p[24:, :HD], p[24:32, HD:])], axis=0)
            )
        wbuf[c, zz, 0, x, l] = heads[0].astype(BF16)
        wbuf[c, zz, 1, x, l] = heads[1].astype(BF16)
        wbuf[c, zz, 2, x, l] = jnp.concatenate(values, axis=1).astype(BF16)
        piece = wbuf.at[c, zz, :, x, l]
        for k in (2, 1, 3):
            cp = remote(piece, piece, xs_sem.at[t, k], xr_sem.at[t, k], device(z, (x + k) % 4, y, c))
            cp.start()
            xcopies.append(cp)

    def along_y(t):
        zz = order[t]
        for k in range(1, 4):
            src = wbuf.at[c, zz, :, (x + 4 - k) % 4, l]
            remote(src, src, xs_sem.at[t, k], xr_sem.at[t, k], other).wait_recv()
        piece = wbuf.at[c, zz, :, :, l]
        cp = remote(piece, piece, ys_sem.at[t], yr_sem.at[t], device(z, x, (y + (1, 7)[t % 2]) % 8, c))
        cp.start()
        ycopies.append(cp)

    def multiply(t, accs):
        zz = order[t]
        dst = wbuf.at[c, zz, :, :, 1 - l]
        remote(dst, dst, ys_sem.at[t], yr_sem.at[t], other).wait_recv()
        cp = remote(wbuf.at[c, zz], wbuf.at[c, zz], ws_sem.at[t], wr_sem.at[zz], other)
        cp.start()
        wcopies.append(cp)
        w0 = wbuf[c, zz, 0].reshape(BLK, 128)
        w1 = wbuf[c, zz, 1].reshape(BLK, 128)
        w2 = wbuf[c, zz, 2].reshape(BLK, 128)
        na = nall[:, pl.ds(pl.multiple_of(2 * zz * BLK, BLK), BLK)]
        nb = nall[:, pl.ds(pl.multiple_of((2 * zz + 1) * BLK, BLK), BLK)]
        return (
            accs[0] + dot(na, jnp.concatenate([w0, w2], axis=1)),
            accs[1] + dot(nb, jnp.concatenate([w1, w2], axis=1)),
        )

    accs = (jnp.zeros((2 * ROWS, 256), F32), jnp.zeros((2 * ROWS, 256), F32))
    along_x(0)
    along_x(1)
    along_x(2)
    along_y(0)
    along_x(3)
    along_y(1)
    along_y(2)
    accs = multiply(0, accs)
    along_y(3)
    for t in range(1, 4):
        accs = multiply(t, accs)
    acc_a, acc_b = accs
    jq = acc_a[:, :128] + acc_b[:, :128]
    jv = acc_a[:, 128:192] + acc_b[:, 192:]
    for i in range(2):
        jpart[i, :, :128] = jq[i * ROWS : (i + 1) * ROWS]
        jpart[i, :, 128:] = jv[i * ROWS : (i + 1) * ROWS]
    jcopy = remote(jpart.at[1 - c], jrecv, jsem.at[0], jsem.at[1], other)
    jcopy.start()
    jcopy.wait_recv()
    joined = jpart[c] + jrecv[...]

    def norm_rows(values):
        centred = values - jnp.mean(values, axis=-1, keepdims=True)
        inverse = lax.rsqrt(jnp.mean(centred * centred, axis=-1, keepdims=True) + EPSILON)
        return centred * inverse, inverse

    normal_q, inverse_q = norm_rows(joined[:, :HD])
    normal_k, inverse_k = norm_rows(joined[:, HD : 2 * HD])
    value = joined[:, 2 * HD :]
    qk_all[0] = jnp.concatenate([normal_q, normal_k], axis=1).astype(BF16)
    v_all[0] = jnp.concatenate([value[:64], value[64:]], axis=1).astype(BF16)
    qcopies = []
    for k in (2, 1, 3):
        for i, buf in enumerate((qk_all, v_all)):
            cp = remote(
                buf.at[0], buf.at[4 - k], qs_sem.at[i, k], qr_sem.at[i, k], device(z, x, (y + 2 * k) % 8, c)
            )
            cp.start()
            qcopies.append(cp)
    id_rows = [
        ids_ref[:, pl.ds(pl.multiple_of(((h + r) % 4) * ROWS, ROWS), ROWS)].astype(F32) for r in range(4)
    ]
    id_row = jnp.concatenate(id_rows, axis=1)
    id_cols = [jnp.broadcast_to(r, (128, 128)).T[:, :1] for r in id_rows]
    for cp in ccopies + qcopies:
        cp.wait_recv()

    qs, ks, vs, cots = [], [], [], []
    for r in range(4):
        both = qk_all[r].astype(F32)
        qs.append(both[:, :HD].astype(BF16))
        ks.append(both[:, HD:].astype(BF16))
        packed = v_all[r].astype(F32)
        vs.append(jnp.concatenate([packed[:, :HD], packed[:, HD:]], axis=0).astype(BF16))
        cots.append(cot_all[r].astype(F32).T)
    k_whole = jnp.concatenate(ks, axis=0)
    v_whole = jnp.concatenate(vs, axis=0)
    factor = 1.0 / math.sqrt(HD)
    key_grad = jnp.zeros((ROWS, HD), F32)
    value_grad = jnp.zeros((ROWS, HD), F32)
    query_grad = None
    for r in range(4):
        scores = dot_nt(qs[r], k_whole) * factor
        expo = jnp.where(id_cols[r] == id_row, jnp.exp(scores), 0.0)
        denom = jnp.sum(expo, axis=-1, keepdims=True)
        probs = expo.astype(BF16)
        attended = dot(probs, v_whole) / denom
        scaled = (cots[r] / denom).astype(BF16)
        correction = jnp.sum(cots[r] * attended, axis=-1, keepdims=True) / denom
        if r == 0:
            out_ref[...] = attended.T.astype(BF16)
            pgrad = dot_nt(scaled, v_whole)
            sgrad = (probs.astype(F32) * (pgrad - correction)).astype(BF16)
            query_grad = dot(sgrad, k_whole) * factor
            sgrad = sgrad[:, :ROWS]
        else:
            pgrad = dot_nt(scaled, vs[0])
            sgrad = (probs[:, :ROWS].astype(F32) * (pgrad - correction)).astype(BF16)
        key_grad += dot_tn(sgrad, qs[r])
        value_grad += dot_tn(probs[:, :ROWS], scaled)
    key_grad = key_grad * factor

    def norm_backward(upstream, normal, inverse):
        shifted = upstream - jnp.mean(upstream, axis=-1, keepdims=True)
        return inverse * (shifted - normal * jnp.mean(upstream * normal, axis=-1, keepdims=True))

    zero = jnp.zeros((ROWS, HD), F32)
    jbuf[c, 0] = jnp.concatenate(
        [norm_backward(query_grad, normal_q, inverse_q), norm_backward(key_grad, normal_k, inverse_k)], axis=1
    ).astype(BF16)
    jbuf[c, 1] = jnp.concatenate([value_grad, zero], axis=1).astype(BF16)
    jbuf[c, 2] = jnp.concatenate([zero, value_grad], axis=1).astype(BF16)
    gcopy = remote(jbuf.at[c], jbuf.at[c], gsem.at[0], gsem.at[1], other)
    gcopy.start()
    theirs = jbuf.at[1 - c]
    remote(theirs, theirs, gsem.at[0], gsem.at[1], other).wait_recv()

    jplanes = [jnp.concatenate([jbuf[0, i], jbuf[1, i]], axis=0) for i in range(3)]
    ja = jnp.concatenate([jplanes[0], jplanes[1]], axis=1)
    jb = jnp.concatenate([jplanes[0], jplanes[2]], axis=1)
    gxcopies = []
    order_t = (2, 1, 3, 0)
    toward = {t: (1, 3)[i % 2] for i, t in enumerate(order_t)}
    for t in order_t:
        zz = (h + t) % 4
        ga = dot(ntr[pl.ds(pl.multiple_of(2 * zz * BLK, BLK), BLK), :], ja)
        gb = dot(ntr[pl.ds(pl.multiple_of((2 * zz + 1) * BLK, BLK), BLK), :], jb)
        gbuf[zz, 0] = ga[:, :128].astype(BF16).reshape(4, 2, 48, 128)
        gbuf[zz, 1] = gb[:, :128].astype(BF16).reshape(4, 2, 48, 128)
        gbuf[zz, 2] = (ga[:, 128:] + gb[:, 128:]).astype(BF16).reshape(4, 2, 48, 128)
        near_x, back_x = (x + toward[t]) % 4, (x + 4 - toward[t]) % 4
        for cp in (
            remote(gbuf.at[zz, :, (x + 2) % 4], relay.at[t], gxs_sem.at[t, 0], gxr_sem.at[t, 0], device(z, near_x, y, c)),
            remote(gbuf.at[zz, :, back_x], xland.at[t, 0], gxs_sem.at[t, 1], gxr_sem.at[t, 1], device(z, back_x, y, c)),
        ):
            cp.start()
            gxcopies.append(cp)

    def merge(t):
        zz = (h + t) % 4
        near_x = (x + toward[t]) % 4
        remote(relay.at[t], relay.at[t], gxs_sem.at[t, 0], gxr_sem.at[t, 0], other).wait_recv()
        msend[t] = (gbuf[zz, :, near_x].astype(F32) + relay[t].astype(F32)).astype(BF16)
        cp = remote(msend.at[t], xland.at[t, 1], gxs_sem.at[t, 2], gxr_sem.at[t, 2], device(z, near_x, y, c))
        cp.start()
        gxcopies.append(cp)

    for cp in wcopies:
        cp.wait_send()
    for zz in range(4):
        dst = wbuf.at[1 - c, zz]
        remote(dst, dst, ws_sem.at[zz], wr_sem.at[zz], other).wait_recv()
    jown_a = jnp.concatenate([jbuf[c, 0], jbuf[c, 1]], axis=1)
    jown_b = jnp.concatenate([jbuf[c, 0], jbuf[c, 2]], axis=1)

    def pg_first(i, carry):
        s1, s2 = carry
        half = i // 4
        zz = i % 4
        w2 = wbuf[half, zz, 2].reshape(BLK, 128)
        mean = stats[0]
        inv = stats[1]
        for ab in range(2):
            wab = wbuf[half, zz, ab].reshape(BLK, 128)
            ng = dot_nt(jown_a if ab == 0 else jown_b, jnp.concatenate([wab, w2], axis=1))
            base = (half * 8 + 2 * zz + ab) * BLK
            for j in range(3):
                col = pl.ds(pl.multiple_of(base + j * 128, 128), 128)
                g = ng[:, j * 128 : (j + 1) * 128]
                hx = (x_ref[:, col].astype(F32) - mean) * inv
                ngs[:, col] = g
                s1 = s1 + g
                s2 = s2 + g * hx
        return s1, s2

    s1 = jnp.zeros((ROWS, 128), F32)
    s2 = s1
    for i in range(8):
        s1, s2 = pg_first(i, (s1, s2))
        if i % 2 == 1:
            merge(order_t[i // 2])
    m1 = jnp.broadcast_to(jnp.sum(s1, axis=-1, keepdims=True) * (1.0 / D), (ROWS, 128))
    m2 = jnp.broadcast_to(jnp.sum(s2, axis=-1, keepdims=True) * (1.0 / D), (ROWS, 128))
    stats[2] = m1
    stats[3] = m2

    gycopies = []
    for t in order_t:
        zz = (h + t) % 4
        total = gbuf[zz, :, x].astype(F32)
        for k in range(2):
            dst = xland.at[t, k]
            remote(dst, dst, gxs_sem.at[t, k + 1], gxr_sem.at[t, k + 1], other).wait_recv()
            total = total + xland[t, k].astype(F32)
        ysend[t] = total.astype(BF16)
        for e in range(2):
            if t == 0 and e == 0:
                continue
            lt = (l + e) % 2
            yt = 2 * zz + lt
            slot = (y - yt + 8) % 8
            cp = remote(
                ysend.at[t, :, lt], yland.at[slot], gys_sem.at[t, e], gyr_sem.at[slot], device(z, x, yt, c)
            )
            cp.start()
            gycopies.append(cp)

    total = ysend[0, :, l].astype(F32)
    for k in range(1, 8):
        dst = yland.at[k]
        remote(dst, dst, gys_sem.at[0, 1], gyr_sem.at[k], other).wait_recv()
        total = total + yland[k].astype(F32)
    tb = total.astype(BF16)
    zsend[0] = tb[0]
    zsend[1] = tb[2]
    zsend[2] = tb[1]
    zsend[3] = tb[2]
    gzcopies = []
    for i in range(2):
        zt = c * 8 + 2 * h + i
        cp = remote(
            zsend.at[pl.ds(2 * i, 2)], zland2.at[z], gzs_sem.at[i], gzr_sem.at[z], device(zt, x, y, c)
        )
        gzcopies.append((zt, cp))

        @pl.when(zt != z)
        def _():
            cp.start()

    def pg_second(i, carry):
        mean = stats[0]
        inv = stats[1]
        m1 = stats[2]
        m2 = stats[3]
        for j in range(3):
            col = pl.ds(pl.multiple_of(i * BLK + j * 128, 128), 128)
            hx = (x_ref[:, col].astype(F32) - mean) * inv
            pg_ref[:, col] = (inv * (ngs[:, col] - m1 - hx * m2)).astype(BF16)
        return carry

    lax.fori_loop(0, 16, pg_second, 0)

    fcopies = []
    for dh in range(4):
        for dc in range(2):
            if dh == 0 and dc == 0:
                continue
            ct = (c + dc) % 2
            fcopies.append(
                remote(
                    fsend.at[ct], fland, fs_sem.at[2 * dh + dc], fr_sem, device(z, x, (y + 2 * dh) % 8, ct)
                )
            )

    @pl.when(own)
    def _():
        second = zlow % 2
        total = zsend[pl.ds(2 * second, 2)].astype(F32)
        for k in (1, 15, 2, 14, 3, 13, 4, 12, 5, 11, 6, 10, 7, 9, 8):
            dst = zland2.at[(z + k) % 16]
            remote(dst, dst, gzs_sem.at[0], gzr_sem.at[(z + k) % 16], other).wait_recv()
            total = total + zland2[(z + k) % 16].astype(F32)
        pair = total[1]
        mine_v = jnp.where(second == 0, pair[:, :HD], pair[:, HD:])
        whole = jnp.concatenate([total[0], mine_v], axis=1)
        fsend[0] = whole[:24]
        fsend[1] = whole[24:]
        for cp in fcopies:
            cp.start()
        gw_ref[...] = fsend[c]
        for cp in fcopies:
            cp.wait_send()

    @pl.when(jnp.logical_not(own))
    def _():
        remote(fland, fland, fs_sem.at[0], fr_sem, other).wait_recv()
        gw_ref[...] = fland[...]

    for cp in zcopies:
        cp.wait_send()

    @pl.when(jnp.logical_not(home))
    def _():
        zcross.wait_send()

    jcopy.wait_send()
    gcopy.wait_send()
    for cp in xcopies + ycopies + ccopies + qcopies + gxcopies + gycopies:
        cp.wait_send()
    for zt, cp in gzcopies:

        @pl.when(zt != z)
        def _():
            cp.wait_send()


def per_device(patches, projection, image_ids, cotangent):
    dma = pltpu.SemaphoreType.DMA
    vmem = pl.BlockSpec(memory_space=pltpu.VMEM)
    scratch = [
        pltpu.VMEM((ROWS, D), BF16),
        pltpu.VMEM((24, 192), BF16),
        pltpu.VMEM((1, 4 * ROWS), jnp.int32),
        pltpu.VMEM((40, 128), BF16),
        pltpu.VMEM((4, 3, 2, 48, 128), BF16),
        pltpu.VMEM((4, 3, 2, 48, 128), BF16),
        dma((7,)),
        pltpu.VMEM((ROWS, D), BF16),
        pltpu.VMEM((2 * ROWS, HALF), BF16),
        pltpu.VMEM((HALF, 2 * ROWS), BF16),
        pltpu.VMEM((4, ROWS, 128), F32),
        pltpu.VMEM((8, 2, 40, 128), BF16),
        pltpu.VMEM((2, 4, 3, 4, 2, 48, 128), BF16),
        pltpu.VMEM((2, ROWS, 192), F32),
        pltpu.VMEM((ROWS, 192), F32),
        pltpu.VMEM((4, ROWS, 128), BF16),
        pltpu.VMEM((4, 64, 128), BF16),
        pltpu.VMEM((4, HD, ROWS), BF16),
        pltpu.VMEM((2, 3, ROWS, 128), BF16),
        pltpu.VMEM((4, 3, 4, 2, 48, 128), BF16),
        pltpu.VMEM((4, 2, 3, 2, 48, 128), BF16),
        pltpu.VMEM((4, 3, 2, 48, 128), BF16),
        pltpu.VMEM((8, 3, 48, 128), BF16),
        pltpu.VMEM((4, 48, 128), BF16),
        pltpu.VMEM((16, 2, 48, 128), BF16),
        pltpu.VMEM((2, 24, 192), F32),
        pltpu.VMEM((24, 192), F32),
        pltpu.VMEM((ROWS, D), F32),
        dma,
        dma((2,)),
        dma((16,)), dma((8, 2)),
        dma((4, 4)), dma((4, 4)),
        dma((4,)), dma((4,)),
        dma((4,)), dma((4,)),
        dma((2,)),
        dma((3, 4)), dma((3, 4)),
        dma((2,)),
        dma((4, 4)), dma((4, 4)),
        dma((4, 2)), dma((8,)),
        dma((2,)), dma((16,)),
        dma((8,)), dma,
    ]
    out, pg, gw = pl.pallas_call(
        kernel,
        out_shape=(
            pltpu.VMEM((HD, ROWS), BF16),
            pltpu.VMEM((ROWS, D), BF16),
            pltpu.VMEM((24, 192), F32),
        ),
        in_specs=[pl.BlockSpec(memory_space=pltpu.HBM)] * 4,
        out_specs=(vmem,) * 3,
        scratch_shapes=scratch,
        compiler_params=pltpu.CompilerParams(
            collective_id=0, has_side_effects=True, vmem_limit_bytes=56 * 2**20
        ),
        name="head",
    )(patches[0], projection, image_ids, cotangent[0].T)
    return out.T[None], pg[None], gw


def solution(mesh):
    in_specs = (P("fsdp", "bal", None), P("fsdp", None), P("fsdp", None), P("fsdp", "bal", None))
    out_specs = (P("fsdp", "bal", None), P("fsdp", "bal", None), P("fsdp", None))
    return jax.shard_map(
        per_device, mesh=mesh, in_specs=in_specs, out_specs=out_specs, check_vma=False
    )
```

```python
import functools
import math

import jax
import jax.numpy as jnp
from jax import lax
from jax.experimental import pallas as pl
from jax.experimental.pallas import tpu as pltpu
from jax.sharding import PartitionSpec as P

EPSILON = 1e-06
MESH = pl.DeviceIdType.MESH
F32 = jnp.float32
BF16 = jnp.bfloat16
NT = (((1,), (1,)), ((), ()))
TN = (((0,), (0,)), ((), ()))

D = 6144
HALF = D // 2
ROWS = 128
HD = 64
BLK = 384


def device(z, x, y, c):
    return (y // 2, ((z * 4 + x) * 2 + y % 2) * 2 + c)


def dot(a, b):
    return jnp.dot(a, b, preferred_element_type=F32)


def dot_nt(a, b):
    return lax.dot_general(a, b, NT, preferred_element_type=F32)


def dot_tn(a, b):
    return lax.dot_general(a, b, TN, preferred_element_type=F32)


def kernel(
    x_hbm, w_hbm, ids_hbm, cot_hbm,
    out_ref, pg_ref, gw_ref,
    x_ref, w_ref, ids_ref, wpack, relay, msend, in_sem, nfull, nall, ntr, stats, zland, wbuf, jpart, jrecv,
    qk_all, v_all, cot_all, jbuf, gbuf, xland, ysend, yland, zsend, zland2, fsend, fland, ngs,
    local_sem, nsem, zs_sem, zr_sem, xs_sem, xr_sem, ys_sem, yr_sem, ws_sem, wr_sem,
    jsem, qs_sem, qr_sem, gsem, gxs_sem, gxr_sem, gys_sem, gyr_sem, gzs_sem, gzr_sem, fs_sem, fr_sem,
):
    h = lax.axis_index("bal")
    f = lax.axis_index("fsdp")
    c = f % 2
    l = (f // 2) % 2
    x = (f // 4) % 4
    z = f // 16
    y = 2 * h + l
    zhalf = z // 8
    zlow = z % 8
    other = device(z, x, y, 1 - c)
    home = zhalf == c
    own = jnp.logical_and(home, zlow // 2 == h)

    def remote(src, dst, ssem, rsem, dev):
        return pltpu.make_async_remote_copy(
            src_ref=src, dst_ref=dst, send_sem=ssem, recv_sem=rsem, device_id=dev, device_id_type=MESH
        )

    loads = [
        pltpu.make_async_copy(x_hbm.at[pl.ds(i * 32, 32)], x_ref.at[pl.ds(i * 32, 32)], in_sem.at[i]) for i in range(4)
    ]
    w_load = pltpu.make_async_copy(w_hbm, w_ref, in_sem.at[4])
    ids_load = pltpu.make_async_copy(ids_hbm, ids_ref, in_sem.at[5])
    cot_load = pltpu.make_async_copy(cot_hbm, cot_all.at[0], in_sem.at[6])
    bar = pltpu.get_barrier_semaphore()

    def signal(dev):
        pl.semaphore_signal(bar, inc=1, device_id=dev, device_id_type=MESH)

    for zl in range(8):
        for cs in range(2):
            me = jnp.logical_and(c * 8 + zl == z, c == cs)

            @pl.when(jnp.logical_not(me))
            def _():
                signal(device(c * 8 + zl, x, y, cs))

    @pl.when(own)
    def _():
        for k in range(1, 16):
            signal(device((z + k) % 16, x, y, c))

    @pl.when(jnp.logical_not(own))
    def _():
        signal(device(z, x, 2 * (zlow // 2) + l, zhalf))

    signal(other)
    for k in range(1, 4):
        signal(device(z, (x + k) % 4, y, c))
    for k in range(1, 8):
        signal(device(z, x, (y + k) % 8, c))
    expected = (
        15 + jnp.where(home, 0, 1) + jnp.where(own, 8, 2) + 1 + 3 + 7
    )

    for cp in [w_load, *loads, ids_load, cot_load]:
        cp.start()

    def norm_body(i, carry):
        rows = pl.ds(pl.multiple_of(i * 16, 16), 16)
        v = x_ref[rows, :].astype(F32)
        mean = jnp.mean(v, axis=-1, keepdims=True)
        cen = v - mean
        inv = lax.rsqrt(jnp.mean(cen * cen, axis=-1, keepdims=True) + EPSILON)
        nfull[rows, :] = (cen * inv).astype(BF16)
        stats[0, rows, :] = jnp.broadcast_to(mean, (16, 128))
        stats[1, rows, :] = jnp.broadcast_to(inv, (16, 128))
        return carry

    w_load.wait()
    wf = w_ref[...].astype(F32)
    wv = wf[:, 128:]
    wpack[...] = jnp.concatenate(
        [wf[:, :128], jnp.concatenate([wv[:16], jnp.concatenate([wv[16:], jnp.zeros((8, HD), F32)], axis=0)], axis=1)],
        axis=0,
    ).astype(BF16)
    for i in range(4):
        loads[i].wait()
        lax.fori_loop(2 * i, 2 * i + 2, norm_body, 0)
    ids_load.wait()
    cot_load.wait()

    pl.semaphore_wait(bar, expected)

    zcopies = []
    for k in (8, 1, 15, 7, 9, 2, 14, 6, 10, 3, 13, 5, 11, 4, 12):
        cp = remote(wpack, zland.at[zlow, c], zs_sem.at[k], zr_sem.at[zlow, c], device((z + k) % 16, x, y, zhalf))
        cp.start()
        zcopies.append(cp)
    zcross = remote(wpack, zland.at[zlow, c], zs_sem.at[0], zr_sem.at[zlow, c], other)

    @pl.when(jnp.logical_not(home))
    def _():
        zcross.start()

    @pl.when(home)
    def _():
        zland[zlow, c] = wpack[...]

    mine = pl.ds(pl.multiple_of(c * ROWS, ROWS), ROWS)
    ncopy = remote(
        nfull.at[:, pl.ds(pl.multiple_of((1 - c) * HALF, HALF), HALF)], nall.at[mine], nsem.at[0], nsem.at[1], other
    )
    ncopy.start()
    nlocal = pltpu.make_async_copy(
        nfull.at[:, pl.ds(pl.multiple_of(c * HALF, HALF), HALF)], nall.at[mine], local_sem
    )
    nlocal.start()
    ccopies = []
    for k in range(1, 4):
        cp = remote(cot_all.at[0], cot_all.at[4 - k], qs_sem.at[2, k], qr_sem.at[2, k], device(z, x, (y + 2 * k) % 8, c))
        cp.start()
        ccopies.append(cp)
    def tr_body(i, carry):
        col = pl.ds(pl.multiple_of(i * BLK, BLK), BLK)
        ntr[col, :] = nall[:, col].T
        return carry

    near = []
    for zz in range(4):
        gap = (z // 2 + 8 - (4 * c + zz)) % 8
        near.append(jnp.minimum(gap, 8 - gap) * 4 + zz)
    ranks = [sum((near[j] < near[i]).astype(jnp.int32) for j in range(4) if j != i) for i in range(4)]
    order = [sum(jnp.where(ranks[i] == t, i, 0) for i in range(4)) for t in range(4)]

    def shard(zl, cs):
        me = jnp.logical_and(c * 8 + zl == z, c == cs)

        @pl.when(jnp.logical_not(me))
        def _():
            remote(wpack, zland.at[zl, cs], zs_sem.at[0], zr_sem.at[zl, cs], other).wait_recv()

        return zland[zl, cs].astype(F32)

    xcopies = []
    ycopies = []
    wcopies = []

    def along_x(t):
        zz = order[t]
        heads, values = [], []
        for zl in (2 * zz, 2 * zz + 1):
            parts = [shard(zl, 0), shard(zl, 1)]
            heads.append(jnp.concatenate([p[:24] for p in parts], axis=0))
            values.append(
                jnp.concatenate([q for p in parts for q in (p[24:, :HD], p[24:32, HD:])], axis=0)
            )
        wbuf[c, zz, 0, x, l] = heads[0].astype(BF16)
        wbuf[c, zz, 1, x, l] = heads[1].astype(BF16)
        wbuf[c, zz, 2, x, l] = jnp.concatenate(values, axis=1).astype(BF16)
        piece = wbuf.at[c, zz, :, x, l]
        for k in (2, 1, 3):
            cp = remote(piece, piece, xs_sem.at[t, k], xr_sem.at[t, k], device(z, (x + k) % 4, y, c))
            cp.start()
            xcopies.append(cp)

    def along_y(t):
        zz = order[t]
        for k in range(1, 4):
            src = wbuf.at[c, zz, :, (x + 4 - k) % 4, l]
            remote(src, src, xs_sem.at[t, k], xr_sem.at[t, k], other).wait_recv()
        for i, step in enumerate((1, 7)):
            piece = wbuf.at[c, zz, :, pl.ds(2 * i, 2), l]
            cp = remote(piece, piece, ys_sem.at[t, i], yr_sem.at[t, i], device(z, x, (y + step) % 8, c))
            cp.start()
            ycopies.append(cp)

    def multiply(t, accs):
        zz = order[t]
        for i in range(2):
            dst = wbuf.at[c, zz, :, pl.ds(2 * i, 2), 1 - l]
            remote(dst, dst, ys_sem.at[t, i], yr_sem.at[t, i], other).wait_recv()
        w0 = wbuf[c, zz, 0].reshape(BLK, 128)
        w1 = wbuf[c, zz, 1].reshape(BLK, 128)
        w2 = wbuf[c, zz, 2].reshape(BLK, 128)
        na = nall[:, pl.ds(pl.multiple_of(2 * zz * BLK, BLK), BLK)]
        nb = nall[:, pl.ds(pl.multiple_of((2 * zz + 1) * BLK, BLK), BLK)]
        return (
            accs[0] + dot(na, jnp.concatenate([w0, w2], axis=1)),
            accs[1] + dot(nb, jnp.concatenate([w1, w2], axis=1)),
        )

    accs = (jnp.zeros((2 * ROWS, 256), F32), jnp.zeros((2 * ROWS, 256), F32))
    along_x(0)
    along_x(1)
    nlocal.wait()
    ncopy.wait()
    lax.fori_loop(0, 2, tr_body, 0)
    along_x(2)
    along_y(0)
    lax.fori_loop(2, 4, tr_body, 0)
    along_x(3)
    along_y(1)
    lax.fori_loop(4, 6, tr_body, 0)
    along_y(2)
    accs = multiply(0, accs)
    along_y(3)
    lax.fori_loop(6, 8, tr_body, 0)
    for t in range(1, 4):
        accs = multiply(t, accs)
    acc_a, acc_b = accs
    jq = acc_a[:, :128] + acc_b[:, :128]
    jv = acc_a[:, 128:192] + acc_b[:, 192:]
    for i in range(2):
        jpart[i, :, :128] = jq[i * ROWS : (i + 1) * ROWS]
        jpart[i, :, 128:] = jv[i * ROWS : (i + 1) * ROWS]
    jcopy = remote(jpart.at[1 - c], jrecv, jsem.at[0], jsem.at[1], other)
    jcopy.start()
    jcopy.wait_recv()
    joined = jpart[c] + jrecv[...]

    def norm_rows(values):
        centred = values - jnp.mean(values, axis=-1, keepdims=True)
        inverse = lax.rsqrt(jnp.mean(centred * centred, axis=-1, keepdims=True) + EPSILON)
        return centred * inverse, inverse

    normal_q, inverse_q = norm_rows(joined[:, :HD])
    normal_k, inverse_k = norm_rows(joined[:, HD : 2 * HD])
    value = joined[:, 2 * HD :]
    qk_all[0] = jnp.concatenate([normal_q, normal_k], axis=1).astype(BF16)
    v_all[0] = jnp.concatenate([value[:64], value[64:]], axis=1).astype(BF16)
    qcopies = []
    for k in (2, 1, 3):
        for i, buf in enumerate((qk_all, v_all)):
            cp = remote(
                buf.at[0], buf.at[4 - k], qs_sem.at[i, k], qr_sem.at[i, k], device(z, x, (y + 2 * k) % 8, c)
            )
            cp.start()
            qcopies.append(cp)
    for zz in range(4):
        cp = remote(wbuf.at[c, zz], wbuf.at[c, zz], ws_sem.at[zz], wr_sem.at[zz], other)
        cp.start()
        wcopies.append(cp)
    id_rows = [
        ids_ref[:, pl.ds(pl.multiple_of(((h + r) % 4) * ROWS, ROWS), ROWS)].astype(F32) for r in range(4)
    ]
    id_row = jnp.concatenate(id_rows, axis=1)
    id_cols = [jnp.broadcast_to(r, (128, 128)).T[:, :1] for r in id_rows]
    id_col = jnp.concatenate(id_cols, axis=0)
    for cp in ccopies:
        cp.wait_recv()
    cots = [cot_all[r].astype(F32).T for r in range(4)]
    for cp in qcopies:
        cp.wait_recv()

    qs, ks, vs = [], [], []
    for r in range(4):
        both = qk_all[r].astype(F32)
        qs.append(both[:, :HD].astype(BF16))
        ks.append(both[:, HD:].astype(BF16))
        packed = v_all[r].astype(F32)
        vs.append(jnp.concatenate([packed[:, :HD], packed[:, HD:]], axis=0).astype(BF16))
    k_whole = jnp.concatenate(ks, axis=0)
    v_whole = jnp.concatenate(vs, axis=0)
    factor = 1.0 / math.sqrt(HD)
    q_whole = jnp.concatenate(qs, axis=0)
    cot_whole = jnp.concatenate(cots, axis=0)
    expo = jnp.where(id_col == id_row, jnp.exp(dot_nt(q_whole, k_whole) * factor), 0.0)
    denom = jnp.sum(expo, axis=-1, keepdims=True)
    probs = expo.astype(BF16)
    attended = dot(probs, v_whole) / denom
    scaled = (cot_whole / denom).astype(BF16)
    correction = jnp.sum(cot_whole * attended, axis=-1, keepdims=True) / denom
    out_ref[...] = attended[:ROWS].T.astype(BF16)
    pgrad = dot_nt(scaled[:ROWS], v_whole)
    sgrad = (probs[:ROWS].astype(F32) * (pgrad - correction[:ROWS])).astype(BF16)
    query_grad = dot(sgrad, k_whole) * factor
    pgrad = dot_nt(scaled, vs[0])
    sgrad = (probs[:, :ROWS].astype(F32) * (pgrad - correction)).astype(BF16)
    key_grad = dot_tn(sgrad, q_whole)
    value_grad = dot_tn(probs[:, :ROWS], scaled)
    key_grad = key_grad * factor

    def norm_backward(upstream, normal, inverse):
        shifted = upstream - jnp.mean(upstream, axis=-1, keepdims=True)
        return inverse * (shifted - normal * jnp.mean(upstream * normal, axis=-1, keepdims=True))

    zero = jnp.zeros((ROWS, HD), F32)
    jbuf[c, 0] = jnp.concatenate(
        [norm_backward(query_grad, normal_q, inverse_q), norm_backward(key_grad, normal_k, inverse_k)], axis=1
    ).astype(BF16)
    jbuf[c, 1] = jnp.concatenate([value_grad, zero], axis=1).astype(BF16)
    jbuf[c, 2] = jnp.concatenate([zero, value_grad], axis=1).astype(BF16)
    gcopy = remote(jbuf.at[c], jbuf.at[c], gsem.at[0], gsem.at[1], other)
    gcopy.start()
    theirs = jbuf.at[1 - c]
    remote(theirs, theirs, gsem.at[0], gsem.at[1], other).wait_recv()

    jplanes = [jnp.concatenate([jbuf[0, i], jbuf[1, i]], axis=0) for i in range(3)]
    ja = jnp.concatenate([jplanes[0], jplanes[1]], axis=1)
    jb = jnp.concatenate([jplanes[0], jplanes[2]], axis=1)
    gxcopies = []
    order_t = (2, 1, 3, 0)
    toward = {t: (1, 3)[i % 2] for i, t in enumerate(order_t)}
    for t in order_t:
        zz = (h + t) % 4
        ga = dot(ntr[pl.ds(pl.multiple_of(2 * zz * BLK, BLK), BLK), :], ja)
        gb = dot(ntr[pl.ds(pl.multiple_of((2 * zz + 1) * BLK, BLK), BLK), :], jb)
        gbuf[zz, 0] = ga[:, :128].astype(BF16).reshape(4, 2, 48, 128)
        gbuf[zz, 1] = gb[:, :128].astype(BF16).reshape(4, 2, 48, 128)
        gbuf[zz, 2] = (ga[:, 128:] + gb[:, 128:]).astype(BF16).reshape(4, 2, 48, 128)
        near_x, back_x = (x + toward[t]) % 4, (x + 4 - toward[t]) % 4
        for cp in (
            remote(gbuf.at[zz, :, (x + 2) % 4], relay.at[t], gxs_sem.at[t, 0], gxr_sem.at[t, 0], device(z, near_x, y, c)),
            remote(gbuf.at[zz, :, back_x], xland.at[t, 0], gxs_sem.at[t, 1], gxr_sem.at[t, 1], device(z, back_x, y, c)),
        ):
            cp.start()
            gxcopies.append(cp)

    def merge(t):
        zz = (h + t) % 4
        near_x = (x + toward[t]) % 4
        remote(relay.at[t], relay.at[t], gxs_sem.at[t, 0], gxr_sem.at[t, 0], other).wait_recv()
        msend[t] = (gbuf[zz, :, near_x].astype(F32) + relay[t].astype(F32)).astype(BF16)
        cp = remote(msend.at[t], xland.at[t, 1], gxs_sem.at[t, 2], gxr_sem.at[t, 2], device(z, near_x, y, c))
        cp.start()
        gxcopies.append(cp)

    for cp in wcopies:
        cp.wait_send()
    for zz in range(4):
        dst = wbuf.at[1 - c, zz]
        remote(dst, dst, ws_sem.at[zz], wr_sem.at[zz], other).wait_recv()
    jown_a = jnp.concatenate([jbuf[c, 0], jbuf[c, 1]], axis=1)
    jown_b = jnp.concatenate([jbuf[c, 0], jbuf[c, 2]], axis=1)

    def pg_first(i, carry):
        s1, s2 = carry
        half = i // 4
        zz = i % 4
        w2 = wbuf[half, zz, 2].reshape(BLK, 128)
        mean = stats[0]
        inv = stats[1]
        for ab in range(2):
            wab = wbuf[half, zz, ab].reshape(BLK, 128)
            ng = dot_nt(jown_a if ab == 0 else jown_b, jnp.concatenate([wab, w2], axis=1))
            base = (half * 8 + 2 * zz + ab) * BLK
            for j in range(3):
                col = pl.ds(pl.multiple_of(base + j * 128, 128), 128)
                g = ng[:, j * 128 : (j + 1) * 128]
                hx = (x_ref[:, col].astype(F32) - mean) * inv
                ngs[:, col] = g
                s1 = s1 + g
                s2 = s2 + g * hx
        return s1, s2

    s1 = jnp.zeros((ROWS, 128), F32)
    s2 = s1
    for i in range(8):
        s1, s2 = pg_first(i, (s1, s2))
        if i % 2 == 1:
            merge(order_t[i // 2])
    m1 = jnp.broadcast_to(jnp.sum(s1, axis=-1, keepdims=True) * (1.0 / D), (ROWS, 128))
    m2 = jnp.broadcast_to(jnp.sum(s2, axis=-1, keepdims=True) * (1.0 / D), (ROWS, 128))
    stats[2] = m1
    stats[3] = m2

    gycopies = []
    for t in order_t:
        zz = (h + t) % 4
        total = gbuf[zz, :, x].astype(F32)
        for k in range(2):
            dst = xland.at[t, k]
            remote(dst, dst, gxs_sem.at[t, k + 1], gxr_sem.at[t, k + 1], other).wait_recv()
            total = total + xland[t, k].astype(F32)
        ysend[t] = total.astype(BF16)
        for e in range(2):
            if t == 0 and e == 0:
                continue
            lt = (l + e) % 2
            yt = 2 * zz + lt
            slot = (y - yt + 8) % 8
            cp = remote(
                ysend.at[t, :, lt], yland.at[slot], gys_sem.at[t, e], gyr_sem.at[slot], device(z, x, yt, c)
            )
            cp.start()
            gycopies.append(cp)

    total = ysend[0, :, l].astype(F32)
    for k in range(1, 8):
        dst = yland.at[k]
        remote(dst, dst, gys_sem.at[0, 1], gyr_sem.at[k], other).wait_recv()
        total = total + yland[k].astype(F32)
    tb = total.astype(BF16)
    zsend[0] = tb[0]
    zsend[1] = tb[2]
    zsend[2] = tb[1]
    zsend[3] = tb[2]
    gzcopies = []
    for i in range(2):
        zt = c * 8 + 2 * h + i
        cp = remote(
            zsend.at[pl.ds(2 * i, 2)], zland2.at[z], gzs_sem.at[i], gzr_sem.at[z], device(zt, x, y, c)
        )
        gzcopies.append((zt, cp))

        @pl.when(zt != z)
        def _():
            cp.start()

    def pg_second(i, carry):
        mean = stats[0]
        inv = stats[1]
        m1 = stats[2]
        m2 = stats[3]
        for j in range(3):
            col = pl.ds(pl.multiple_of(i * BLK + j * 128, 128), 128)
            hx = (x_ref[:, col].astype(F32) - mean) * inv
            pg_ref[:, col] = (inv * (ngs[:, col] - m1 - hx * m2)).astype(BF16)
        return carry

    lax.fori_loop(0, 16, pg_second, 0)

    fcopies = []
    for dh in range(4):
        for dc in range(2):
            if dh == 0 and dc == 0:
                continue
            ct = (c + dc) % 2
            fcopies.append(
                remote(
                    fsend.at[ct], fland, fs_sem.at[2 * dh + dc], fr_sem, device(z, x, (y + 2 * dh) % 8, ct)
                )
            )

    @pl.when(own)
    def _():
        second = zlow % 2
        total = zsend[pl.ds(2 * second, 2)].astype(F32)
        for k in (1, 15, 2, 14, 3, 13, 4, 12, 5, 11, 6, 10, 7, 9, 8):
            dst = zland2.at[(z + k) % 16]
            remote(dst, dst, gzs_sem.at[0], gzr_sem.at[(z + k) % 16], other).wait_recv()
            total = total + zland2[(z + k) % 16].astype(F32)
        pair = total[1]
        mine_v = jnp.where(second == 0, pair[:, :HD], pair[:, HD:])
        whole = jnp.concatenate([total[0], mine_v], axis=1)
        fsend[0] = whole[:24]
        fsend[1] = whole[24:]
        for cp in fcopies:
            cp.start()
        gw_ref[...] = fsend[c]
        for cp in fcopies:
            cp.wait_send()

    @pl.when(jnp.logical_not(own))
    def _():
        remote(fland, fland, fs_sem.at[0], fr_sem, other).wait_recv()
        gw_ref[...] = fland[...]

    for cp in zcopies:
        cp.wait_send()

    @pl.when(jnp.logical_not(home))
    def _():
        zcross.wait_send()

    jcopy.wait_send()
    gcopy.wait_send()
    for cp in xcopies + ycopies + ccopies + qcopies + gxcopies + gycopies:
        cp.wait_send()
    for zt, cp in gzcopies:

        @pl.when(zt != z)
        def _():
            cp.wait_send()


def per_device(patches, projection, image_ids, cotangent):
    dma = pltpu.SemaphoreType.DMA
    vmem = pl.BlockSpec(memory_space=pltpu.VMEM)
    scratch = [
        pltpu.VMEM((ROWS, D), BF16),
        pltpu.VMEM((24, 192), BF16),
        pltpu.VMEM((1, 4 * ROWS), jnp.int32),
        pltpu.VMEM((40, 128), BF16),
        pltpu.VMEM((4, 3, 2, 48, 128), BF16),
        pltpu.VMEM((4, 3, 2, 48, 128), BF16),
        dma((7,)),
        pltpu.VMEM((ROWS, D), BF16),
        pltpu.VMEM((2 * ROWS, HALF), BF16),
        pltpu.VMEM((HALF, 2 * ROWS), BF16),
        pltpu.VMEM((4, ROWS, 128), F32),
        pltpu.VMEM((8, 2, 40, 128), BF16),
        pltpu.VMEM((2, 4, 3, 4, 2, 48, 128), BF16),
        pltpu.VMEM((2, ROWS, 192), F32),
        pltpu.VMEM((ROWS, 192), F32),
        pltpu.VMEM((4, ROWS, 128), BF16),
        pltpu.VMEM((4, 64, 128), BF16),
        pltpu.VMEM((4, HD, ROWS), BF16),
        pltpu.VMEM((2, 3, ROWS, 128), BF16),
        pltpu.VMEM((4, 3, 4, 2, 48, 128), BF16),
        pltpu.VMEM((4, 2, 3, 2, 48, 128), BF16),
        pltpu.VMEM((4, 3, 2, 48, 128), BF16),
        pltpu.VMEM((8, 3, 48, 128), BF16),
        pltpu.VMEM((4, 48, 128), BF16),
        pltpu.VMEM((16, 2, 48, 128), BF16),
        pltpu.VMEM((2, 24, 192), F32),
        pltpu.VMEM((24, 192), F32),
        pltpu.VMEM((ROWS, D), F32),
        dma,
        dma((2,)),
        dma((16,)), dma((8, 2)),
        dma((4, 4)), dma((4, 4)),
        dma((4, 2)), dma((4, 2)),
        dma((4,)), dma((4,)),
        dma((2,)),
        dma((3, 4)), dma((3, 4)),
        dma((2,)),
        dma((4, 4)), dma((4, 4)),
        dma((4, 2)), dma((8,)),
        dma((2,)), dma((16,)),
        dma((8,)), dma,
    ]
    out, pg, gw = pl.pallas_call(
        kernel,
        out_shape=(
            pltpu.VMEM((HD, ROWS), BF16),
            pltpu.VMEM((ROWS, D), BF16),
            pltpu.VMEM((24, 192), F32),
        ),
        in_specs=[pl.BlockSpec(memory_space=pltpu.HBM)] * 4,
        out_specs=(vmem,) * 3,
        scratch_shapes=scratch,
        compiler_params=pltpu.CompilerParams(
            collective_id=0, has_side_effects=True, vmem_limit_bytes=56 * 2**20
        ),
        name="head",
    )(patches[0], projection, image_ids, cotangent[0].T)
    return out.T[None], pg[None], gw


def solution(mesh):
    in_specs = (P("fsdp", "bal", None), P("fsdp", None), P("fsdp", None), P("fsdp", "bal", None))
    out_specs = (P("fsdp", "bal", None), P("fsdp", "bal", None), P("fsdp", None))
    return jax.shard_map(
        per_device, mesh=mesh, in_specs=in_specs, out_specs=out_specs, check_vma=False
    )
```
